32 devices in a mesh: user: 8 (over z, x), tp: 4 (over y, core).
Axes of the slice: x: 2, y: 2, z: 4, core: 2. Of those that a mesh axis runs over, the one named last changes fastest.
Arguments:
- cand_feats: bfloat16 [8192, 1024], P('user', 'tp'), may hold values from -6 to 6
- w_in: bfloat16 [1024, 2048], P(None, 'tp'), may hold values from -0.1875 to 0.1875
- w_out: bfloat16 [1024, 1024], P('tp'), may hold values from -0.1875 to 0.1875
- kv_cache: bfloat16 [512, 128, 2048], P('user', None, 'tp'), may hold values from -6 to 6
- event_mask: int32 [512, 128], P('user'), may hold values from 0 to 1, as said below
- block_counts: int32 [64], P('user'), may hold values from 1 to 8, as said below
- user_blocks: int32 [64, 8], P('user'), may hold values from 0 to 63, as said below
- send_slots: int32 [64, 8], P('user'), may hold values from 0 to 63, as said below
- cand_user: int32 [8192], P('user'), may hold values from 0 to 7
Outputs:
- scored: bfloat16 [8192, 1024], P('user', 'tp')
The draws below stay inside these ranges and needn't reach their ends.
Inputs may be any that keep to these rules, and one draw needn't show every extreme that they name: `block_counts`: on every index of the user axis some user has 8 blocks, and on one index every user has. For user u of the index r of the user axis and j < block_counts[r * 8 + u], user_blocks[r * 8 + u, j] = o * 8 + c says that block j of u's history is cached on index o, in its local row send_slots[o * 8 + r, c] of kv_cache and event_mask. These valid entries of one index's users are all different, and on one index they take all 64 values. Entries with j >= block_counts[u] are arbitrary. `send_slots`: the 8 rows of one holder o (rows o * 8 to o * 8 + 7) name each of its local rows 0 to 63 exactly once. `event_mask`: in every block of a user's history the first event is real.
All inputs are finite; a program needn't handle non-finite values.
Results may differ from the reference program's by a relative error of at most 0.013.
Values may be sent and summed in bfloat16 or wider, within the bound.
No kernel may reach another device: no remote copies, remote signals or barrier semaphores. Data moves between devices by JAX's collectives and lax.ppermute only.
A program may use at most 128 MiB of HBM per device.

```python
import jax
import jax.numpy as jnp
from jax import lax

D = 1024
H = 8
DH = 128
EVENTS = 128
MAXB = 8
USERS_DEV = 8
CAND_DEV = 1024
CAP = 8
SLOTS = 64
BLOCKS = 512
CANDS = 8192
N_USER = 8


def shuffle_peers(subkey):
    return jax.random.permutation(subkey, N_USER)


def shuffle_slots(subkey):
    return jax.random.permutation(subkey, SLOTS)


def make_tables(key):
    base_key = jax.random.fold_in(key, 4243)
    keyset = jax.random.split(base_key, 10)
    peer_count = N_USER
    most_blocks = MAXB
    draw_first = jax.random.randint(keyset[0], (peer_count, USERS_DEV), 1, most_blocks + 1)
    draw_second = jax.random.randint(keyset[1], (peer_count, USERS_DEV), 1, most_blocks + 1)
    counts = (draw_first * draw_second + most_blocks - 1) // most_blocks
    full_user = jax.random.randint(keyset[2], (peer_count,), 0, USERS_DEV)
    user_ids = jnp.arange(USERS_DEV)
    counts = jnp.where(user_ids[None, :] == full_user[:, None], most_blocks, counts)
    full_rank = jax.random.randint(keyset[3], (), 0, peer_count)
    counts = jnp.where(jnp.arange(peer_count)[:, None] == full_rank, most_blocks, counts)
    offsets = jnp.cumsum(counts, axis=1) - counts
    block_pos = jnp.arange(most_blocks)
    sequence_no = offsets[:, :, None] + block_pos[None, None, :]
    in_use = block_pos[None, None, :] < counts[:, :, None]
    spreads = jax.vmap(shuffle_peers)(jax.random.split(keyset[4], peer_count))
    owners = jnp.take_along_axis(spreads, (sequence_no % peer_count).reshape(peer_count, -1), axis=1).reshape(sequence_no.shape)
    places = sequence_no // peer_count
    garbage = jax.random.randint(keyset[5], sequence_no.shape, 0, peer_count * CAP)
    blocks_table = jnp.where(in_use, owners * CAP + places, garbage)
    slot_perm = jax.vmap(shuffle_slots)(jax.random.split(keyset[6], peer_count))
    last_len = jax.random.randint(keyset[7], (peer_count, USERS_DEV), 1, EVENTS + 1)
    lengths = jnp.where(block_pos[None, None, :] == counts[:, :, None] - 1, last_len[:, :, None], EVENTS)
    events = jnp.arange(EVENTS)
    hole_draw = jax.random.randint(keyset[8], sequence_no.shape + (EVENTS,), 0, 4)
    kept_mask = ((events < lengths[..., None]) & ((hole_draw > 0) | (events == 0))).astype(jnp.int32)
    filler = jax.random.randint(keyset[9], (peer_count, peer_count, CAP, EVENTS), 0, 2)
    rank_ids = jnp.broadcast_to(jnp.arange(peer_count)[:, None, None], sequence_no.shape)
    target = jnp.where(in_use, places, CAP)
    mask_grid = filler.at[rank_ids, owners, target].set(kept_mask, mode='drop')
    by_owner = jnp.transpose(mask_grid, (1, 0, 2, 3)).reshape(peer_count, SLOTS, EVENTS)
    mask_rows = jnp.zeros((peer_count, SLOTS, EVENTS), jnp.int32).at[jnp.arange(peer_count)[:, None], slot_perm].set(by_owner)
    return (counts.reshape(-1).astype(jnp.int32), blocks_table.reshape(peer_count * USERS_DEV, most_blocks).astype(jnp.int32), slot_perm.reshape(peer_count * peer_count, CAP).astype(jnp.int32), mask_rows.reshape(peer_count * SLOTS, EVENTS).astype(jnp.int32))


def draw_block_counts(key, part):
    return make_tables(key)[0]


def draw_user_blocks(key, part):
    return make_tables(key)[1]


def draw_send_slots(key, part):
    return make_tables(key)[2]


def draw_event_mask(key, part):
    return make_tables(key)[3]


def set_ends(array, rng, low, largest):
    longest = array.shape.index(max(array.shape))
    spots = []
    for shift in (0, 1):
        where = [jax.random.randint(jax.random.fold_in(rng, axis), (), 0, length) for axis, length in enumerate(array.shape)]
        where[longest] = (where[longest] + shift) % array.shape[longest]
        spots.append(tuple(where))
    return array.at[spots[0]].set(low).at[spots[1]].set(largest)


def steps_of(own_key, dims, pieces, smallest, high):
    loudness, own = 1.0, jax.random.fold_in(own_key, 6)
    for position, blocks in pieces:
        draws = jnp.exp(jax.random.uniform(jax.random.fold_in(own, position), (blocks,), jnp.float32, smallest / len(pieces), high / len(pieces)))
        loudness = loudness * jnp.repeat(draws, dims[position] // blocks).reshape([-1 if axis == position else 1 for axis in range(len(dims))])
    return loudness


def noise(rng, shape, width, reach, pieces=(), held_as=jnp.bfloat16):
    loudness = steps_of(rng, shape, pieces, -0.22, 0.18) if pieces else 1.0
    values = jax.random.normal(rng, shape, jnp.float32) * width * loudness
    return jnp.minimum(jnp.maximum(values, -reach), reach).astype(held_as)


def setup_inputs(seed: int = 0) -> dict:
    key_list = jax.random.split(jax.random.key(seed), 10)
    cand_feats = noise(key_list[0], (CANDS, D), 1.0, 6.0, ((0, 8), (1, 4)))
    w_in = noise(key_list[1], (D, 2 * D), D ** -0.5, 0.1875, ((1, 4),))
    w_out = noise(key_list[2], (D, D), D ** -0.5, 0.1875, ((0, 4),))
    kv_cache = noise(key_list[3], (BLOCKS, EVENTS, 2 * D), 1.0, 6.0, ((0, 8), (2, 4)))
    event_mask = draw_event_mask(jax.random.fold_in(key_list[9], 71), 0)
    block_counts = draw_block_counts(jax.random.fold_in(key_list[9], 71), 0)
    user_blocks = draw_user_blocks(jax.random.fold_in(key_list[9], 71), 0)
    send_slots = draw_send_slots(jax.random.fold_in(key_list[9], 71), 0)
    cand_user = set_ends(jax.random.randint(key_list[8], (CANDS,), 0, USERS_DEV), jax.random.fold_in(key_list[8], 1), 0, USERS_DEV - 1).astype(jnp.int32)
    return {"cand_feats": cand_feats, "w_in": w_in, "w_out": w_out, "kv_cache": kv_cache, "event_mask": event_mask, "block_counts": block_counts, "user_blocks": user_blocks, "send_slots": send_slots, "cand_user": cand_user}


norm_eps = 1e-06

def owner_users(block_count, block_table, slot_count):
    user_count, most_blocks = block_table.shape
    live_mask = jnp.arange(most_blocks, dtype=jnp.int32)[None, :] < block_count[:, None]
    slot_hit = (block_table[:, :, None] == jnp.arange(slot_count, dtype=jnp.int32)[None, None, :]) & live_mask[:, :, None]
    user_label = jnp.arange(user_count, dtype=jnp.int32)[:, None, None] + 1
    return (lax.optimization_barrier(jnp.sum(jnp.where(slot_hit, user_label, 0), axis=(0, 1))) - 1).astype(jnp.int32)

def attend_ref(queries, cand_users, key_rows, value_rows, live_mask, slot_users):
    block_rows = min(512, CAND_DEV)
    key_float = key_rows.astype(jnp.float32)
    value_float = value_rows.astype(jnp.float32)

    def one_block(packed):
        query_block, user_block = packed
        same_user = (user_block[:, None] == slot_users[None, :]).astype(jnp.float32)
        weights = (same_user[:, :, None] * live_mask[None]).reshape(query_block.shape[0], -1)
        scores = jnp.einsum('rhd,ehd->hre', query_block.astype(jnp.float32), key_float) * DH ** (-0.5)
        attn_weights = (jax.nn.silu(scores) * weights[None]).astype(jnp.bfloat16)
        return jnp.einsum('hre,ehd->rhd', attn_weights.astype(jnp.float32), value_float)
    result = lax.map(one_block, (queries.reshape(-1, block_rows, H, DH), cand_users.reshape(-1, block_rows)))
    return result.reshape(-1, H, DH)

def reference(cand_feats, w_in, w_out, kv_cache, event_mask, block_counts, user_blocks, send_slots, cand_user):
    slot_total = N_USER * CAP
    slot_table = send_slots.reshape(N_USER, N_USER, CAP)

    def ranker(ranker_index):
        features = lax.dynamic_slice_in_dim(cand_feats, ranker_index * CAND_DEV, CAND_DEV, 0)
        users_here = lax.dynamic_slice_in_dim(cand_user, ranker_index * CAND_DEV, CAND_DEV, 0)
        counts_here = lax.dynamic_slice_in_dim(block_counts, ranker_index * USERS_DEV, USERS_DEV, 0)
        table_here = lax.dynamic_slice_in_dim(user_blocks, ranker_index * USERS_DEV, USERS_DEV, 0)
        projected = jnp.dot(features, w_in, preferred_element_type=jnp.float32)
        activated = jax.nn.silu(projected).reshape(CAND_DEV, H, 2, DH)
        queries = activated[:, :, 0, :].astype(jnp.bfloat16)
        gates = activated[:, :, 1, :].astype(jnp.bfloat16)
        picked = jnp.take(slot_table, ranker_index, axis=1).astype(jnp.int32)
        global_rows = (jnp.arange(N_USER, dtype=jnp.int32)[:, None] * SLOTS + picked).reshape(-1).astype(jnp.int32)
        blocks_here = kv_cache[global_rows].reshape(slot_total * EVENTS, H, 2, DH)
        live_mask = event_mask[global_rows].astype(jnp.float32)
        slot_users = owner_users(counts_here, table_here, slot_total)
        attended = attend_ref(queries, users_here, blocks_here[:, :, 0, :], blocks_here[:, :, 1, :], live_mask, slot_users)
        normed = attended * lax.rsqrt(lax.optimization_barrier(jnp.mean(attended * attended, axis=-1, keepdims=True)) + norm_eps) * gates.astype(jnp.float32)
        hidden = normed.astype(jnp.bfloat16).reshape(CAND_DEV, H * DH)
        mixed = jnp.dot(hidden, w_out, preferred_element_type=jnp.float32)
        return (features.astype(jnp.float32) + mixed).astype(jnp.bfloat16)
    scored = lax.map(ranker, jnp.arange(N_USER, dtype=jnp.int32))
    return scored.reshape(CANDS, D)
```

```python
import functools

import jax
import jax.numpy as jnp
from jax import lax
from jax.experimental import pallas as pl
from jax.experimental.pallas import tpu as pltpu
from jax.sharding import PartitionSpec as P

DH = 128
EVENTS = 128
norm_eps = 1e-06
MASKED = -1e30


def ring_order(count):
    wide = 1
    while 4 * wide * wide <= count:
        wide *= 2
    deep = count // wide
    order = [z * wide for z in range(deep)]
    for turn, z in enumerate(reversed(range(deep))):
        across = range(1, wide) if turn % 2 == 0 else reversed(range(1, wide))
        order += [z * wide + x for x in across]
    return order


def owner_users(block_count, block_table, slot_count):
    user_count, most_blocks = block_table.shape
    live_mask = jnp.arange(most_blocks, dtype=jnp.int32)[None, :] < block_count[:, None]
    slot_hit = (
        block_table[:, :, None] == jnp.arange(slot_count, dtype=jnp.int32)[None, None, :]
    ) & live_mask[:, :, None]
    user_label = jnp.arange(user_count, dtype=jnp.int32)[:, None, None] + 1
    return jnp.sum(jnp.where(slot_hit, user_label, 0), axis=(0, 1)) - 1


def attend_kernel(
    heads, cap, table, q_a, q_b, onehot, penalty, cache, out_a, out_b, kv, hot, pen, sems
):
    rows = q_a.shape[0]
    copies = []
    for d in range(2):
        index = table[d]
        mine = [
            pltpu.make_async_copy(
                onehot.at[index, pl.ds(d * rows, rows)], hot.at[d], sems.at[d, cap]
            ),
            pltpu.make_async_copy(penalty.at[index], pen.at[d], sems.at[d, cap + 1]),
        ]
        for c in range(cap):
            mine.append(
                pltpu.make_async_copy(
                    cache.at[table[2 + d * cap + c]],
                    kv.at[d, pl.ds(c * EVENTS, EVENTS)],
                    sems.at[d, c],
                )
            )
        for copy in mine:
            copy.start()
        copies.append(mine)
    tile = min(256, rows)
    events = cap * EVENTS
    chunk = min(256, events)
    for d, (q, out) in enumerate(((q_a, out_a), (q_b, out_b))):
        for copy in copies[d]:
            copy.wait()
        for h in range(heads):
            for t in range(0, rows, tile):
                left = jnp.concatenate(
                    [q[t : t + tile, h * DH : (h + 1) * DH], hot[d, t : t + tile]], axis=1
                )
                total = jnp.zeros((tile, DH), jnp.float32)
                for e in range(0, events, chunk):
                    right = jnp.concatenate(
                        [
                            kv[d, e : e + chunk, 2 * h * DH : (2 * h + 1) * DH],
                            pen[d, e : e + chunk],
                        ],
                        axis=1,
                    )
                    half = lax.dot_general(
                        left, right, (((1,), (1,)), ((), ())), preferred_element_type=jnp.float32
                    ) * (0.5 * DH ** (-0.5))
                    weights = (half + half * jnp.tanh(half)).astype(jnp.bfloat16)
                    total += jnp.dot(
                        weights,
                        kv[d, e : e + chunk, (2 * h + 1) * DH : (2 * h + 2) * DH],
                        preferred_element_type=jnp.float32,
                    )
                out[t : t + tile, h * DH : (h + 1) * DH] = total


def attend(table, q_a, q_b, onehot, penalty, cache, heads, cap):
    rows = q_a.shape[0]
    events = cap * EVENTS
    vmem = pl.BlockSpec(memory_space=pltpu.VMEM)
    hbm = pl.BlockSpec(memory_space=pl.ANY)
    out = jax.ShapeDtypeStruct((rows, heads * DH), jnp.float32)
    return pl.pallas_call(
        functools.partial(attend_kernel, heads, cap),
        out_shape=(out, out),
        in_specs=[pl.BlockSpec(memory_space=pltpu.SMEM), vmem, vmem, hbm, hbm, hbm],
        out_specs=(vmem, vmem),
        scratch_shapes=[
            pltpu.VMEM((2, events, 2 * heads * DH), jnp.bfloat16),
            pltpu.VMEM((2, rows, DH), jnp.bfloat16),
            pltpu.VMEM((2, events, DH), jnp.bfloat16),
            pltpu.SemaphoreType.DMA((2, cap + 2)),
        ],
        compiler_params=pltpu.CompilerParams(vmem_limit_bytes=24 * 1024 * 1024),
        cost_estimate=pl.CostEstimate(
            flops=2 * 2 * 3 * rows * events * heads * DH,
            bytes_accessed=2 * (events * heads * 4 * DH + events * 2 * DH + rows * heads * DH * 6),
            transcendentals=2 * rows * events * heads,
        ),
        name="attend",
    )(table, q_a, q_b, onehot, penalty, cache)


def per_device(
    cand_feats, w_in, w_out, kv_cache, event_mask, block_counts, user_blocks, send_slots, cand_user
):
    row_count, slice_width = cand_feats.shape
    heads = w_out.shape[0] // DH
    peers = lax.axis_size("user")
    parts = lax.axis_size("tp")
    cap = send_slots.shape[1]
    me = lax.axis_index("user")
    part = lax.axis_index("tp")
    half = row_count // 2

    order = ring_order(peers)
    place = [0] * peers
    for position, index in enumerate(order):
        place[index] = position
    here = jnp.array(place, jnp.int32)[me]
    onward = [(order[i], order[(i + 1) % peers]) for i in range(peers)]
    back = [(b, a) for a, b in onward]

    def swap(value, bit):
        return lax.ppermute(value, "tp", [(t, t ^ bit) for t in range(parts)])

    bits = [1 << b for b in range(parts.bit_length() - 1)]

    slices = {0: cand_feats}
    for bit in reversed(bits):
        slices.update({m | bit: swap(value, bit) for m, value in list(slices.items())})
    features = jnp.concatenate([slices[m] for m in range(parts)], axis=1)
    w_rows = jnp.concatenate(
        [
            lax.dynamic_slice_in_dim(w_in, (part ^ m) * slice_width, slice_width, 0)
            for m in range(parts)
        ],
        axis=0,
    ).reshape(-1, heads, 2, DH)
    w_query = w_rows[:, :, 0].reshape(-1, heads * DH)
    w_gate = w_rows[:, :, 1].reshape(-1, heads * DH)
    out_columns = [
        lax.dynamic_slice_in_dim(w_out, (part ^ m) * slice_width, slice_width, 1)
        for m in range(parts)
    ]

    slot_users = owner_users(block_counts, user_blocks, peers * cap)
    facts = lax.all_gather(jnp.concatenate([cand_user, slot_users]), "user", axis=0)
    users, owners = facts[:, :row_count], facts[:, row_count:]
    onehot = (users[:, :, None] == jnp.arange(DH, dtype=jnp.int32)).astype(jnp.bfloat16)
    my_owners = lax.dynamic_slice_in_dim(owners, me * cap, cap, 1)
    live = event_mask[send_slots.reshape(-1)].reshape(peers, cap, EVENTS) > 0
    label = jnp.where(live, my_owners[:, :, None], -1).reshape(peers, cap * EVENTS)
    penalty = jnp.where(
        label[:, :, None] == jnp.arange(DH, dtype=jnp.int32), 0.0, MASKED
    ).astype(jnp.bfloat16)

    steps = jnp.arange(peers, dtype=jnp.int32)
    sequence = jnp.array(order, jnp.int32)
    met = jnp.stack([sequence[(here - steps) % peers], sequence[(here + steps) % peers]], axis=1)
    tables = jnp.concatenate([met, send_slots[met].reshape(peers, 2 * cap)], axis=1)

    queries = jax.nn.silu(
        jnp.dot(features, w_query, preferred_element_type=jnp.float32)
    ).astype(jnp.bfloat16)
    gates = jax.nn.silu(
        jnp.dot(features, w_gate, preferred_element_type=jnp.float32)
    ).astype(jnp.bfloat16)

    def score(step, q_a, q_b):
        return attend(tables[step], q_a, q_b, onehot, penalty, kv_cache, heads, cap)

    q_a, q_b = queries[:half], queries[half:]
    own_a, own_b = score(0, q_a, q_b)
    sum_a = sum_b = None
    for step in range(1, peers):
        q_a = lax.ppermute(q_a, "user", onward)
        q_b = lax.ppermute(q_b, "user", back)
        term_a, term_b = score(step, q_a, q_b)
        if sum_a is not None:
            term_a += sum_a.astype(jnp.float32)
            term_b += sum_b.astype(jnp.float32)
        sum_a = lax.ppermute(term_a.astype(jnp.bfloat16), "user", onward)
        sum_b = lax.ppermute(term_b.astype(jnp.bfloat16), "user", back)
    attended = jnp.concatenate(
        [own_a + sum_a.astype(jnp.float32), own_b + sum_b.astype(jnp.float32)], axis=0
    ).reshape(row_count, heads, DH)
    normed = (
        attended
        * lax.rsqrt(jnp.mean(attended * attended, axis=-1, keepdims=True) + norm_eps)
        * gates.reshape(row_count, heads, DH).astype(jnp.float32)
    )
    hidden = normed.astype(jnp.bfloat16).reshape(row_count, heads * DH)
    terms = {
        m: jnp.dot(hidden, out_columns[m], preferred_element_type=jnp.float32)
        for m in range(parts)
    }
    for bit in bits:
        for m in [m for m in terms if m & bit]:
            terms[m ^ bit] += swap(terms.pop(m).astype(jnp.bfloat16), bit).astype(jnp.float32)
    return (cand_feats.astype(jnp.float32) + terms[0]).astype(jnp.bfloat16)


def solution(mesh):
    in_specs = (
        P("user", "tp"),
        P(None, "tp"),
        P("tp", None),
        P("user", None, "tp"),
        P("user", None),
        P("user"),
        P("user", None),
        P("user", None),
        P("user"),
    )
    out_specs = P("user", "tp")
    return jax.shard_map(
        per_device, mesh=mesh, in_specs=in_specs, out_specs=out_specs, check_vma=False
    )
```

```python
import functools

import jax
import jax.numpy as jnp
from jax import lax
from jax.experimental import pallas as pl
from jax.experimental.pallas import tpu as pltpu
from jax.sharding import PartitionSpec as P

DH = 128
EVENTS = 128
norm_eps = 1e-06
MASKED = -1e30

VMEM = pl.BlockSpec(memory_space=pltpu.VMEM)
SMEM = pl.BlockSpec(memory_space=pltpu.SMEM)


def pinned(*values):
    return [pltpu.with_memory_space_constraint(value, pltpu.VMEM) for value in values]


def ring_order(count):
    wide = 1
    while 4 * wide * wide <= count:
        wide *= 2
    deep = count // wide
    order = [z * wide for z in range(deep)]
    for turn, z in enumerate(reversed(range(deep))):
        across = range(1, wide) if turn % 2 == 0 else reversed(range(1, wide))
        order += [z * wide + x for x in across]
    return order


def owner_users(block_count, block_table, slot_count):
    user_count, most_blocks = block_table.shape
    live_mask = jnp.arange(most_blocks, dtype=jnp.int32)[None, :] < block_count[:, None]
    slot_hit = (
        block_table[:, :, None] == jnp.arange(slot_count, dtype=jnp.int32)[None, None, :]
    ) & live_mask[:, :, None]
    user_label = jnp.arange(user_count, dtype=jnp.int32)[:, None, None] + 1
    return jnp.sum(jnp.where(slot_hit, user_label, 0), axis=(0, 1)) - 1


def silu(value):
    return value * (0.5 + 0.5 * jnp.tanh(0.5 * value))


def project_kernel(heads, gate, part, *refs):
    *slices, w_in, out = refs
    width = slices[0].shape[1]
    for h in range(heads):
        column = (2 * h + gate) * DH
        total = None
        for m, piece in enumerate(slices):
            start = pl.multiple_of((part[0] ^ m) * width, width)
            term = jnp.dot(
                piece[...],
                w_in[pl.ds(start, width), column : column + DH],
                preferred_element_type=jnp.float32,
            )
            total = term if total is None else total + term
        out[:, h * DH : (h + 1) * DH] = silu(total).astype(jnp.bfloat16)


def project(part, slices, w_in, heads, gate):
    rows, width = slices[0].shape
    return pl.pallas_call(
        functools.partial(project_kernel, heads, gate),
        out_shape=jax.ShapeDtypeStruct((rows, heads * DH), jnp.bfloat16),
        in_specs=[SMEM] + [VMEM] * (len(slices) + 1),
        out_specs=VMEM,
        compiler_params=pltpu.CompilerParams(vmem_limit_bytes=16 * 1024 * 1024),
        cost_estimate=pl.CostEstimate(
            flops=2 * rows * width * len(slices) * heads * DH,
            bytes_accessed=2 * rows * width * len(slices),
            transcendentals=rows * heads * DH,
        ),
        name="gates" if gate else "queries",
    )(part, *pinned(*slices, w_in))


def attend_kernel(heads, cap, table, q_a, q_b, onehot, penalty, cache, out_a, out_b):
    rows = q_a.shape[0]
    per = min(2, cap)
    for d, (q, out) in enumerate(((q_a, out_a), (q_b, out_b))):
        index = table[d]
        hot = onehot[index, d * rows : (d + 1) * rows]
        for h in range(heads):
            left = jnp.concatenate([q[:, h * DH : (h + 1) * DH], hot], axis=1)
            total = None
            for c in range(0, cap, per):
                held = [cache.at[table[2 + d * cap + c + i]] for i in range(per)]
                keys = jnp.concatenate([b[:, 2 * h * DH : (2 * h + 1) * DH] for b in held], axis=0)
                values = jnp.concatenate(
                    [b[:, (2 * h + 1) * DH : (2 * h + 2) * DH] for b in held], axis=0
                )
                right = jnp.concatenate(
                    [keys, penalty[index, c * EVENTS : (c + per) * EVENTS]], axis=1
                )
                half = lax.dot_general(
                    left, right, (((1,), (1,)), ((), ())), preferred_element_type=jnp.float32
                ) * (0.5 * DH ** (-0.5))
                weights = (half + half * jnp.tanh(half)).astype(jnp.bfloat16)
                term = jnp.dot(weights, values, preferred_element_type=jnp.float32)
                total = term if total is None else total + term
            out[:, h * DH : (h + 1) * DH] = total


def attend(table, q_a, q_b, onehot, penalty, cache, heads, cap):
    rows = q_a.shape[0]
    events = cap * EVENTS
    out = jax.ShapeDtypeStruct((rows, heads * DH), jnp.float32)
    return pl.pallas_call(
        functools.partial(attend_kernel, heads, cap),
        out_shape=(out, out),
        in_specs=[SMEM] + [VMEM] * 5,
        out_specs=(VMEM, VMEM),
        compiler_params=pltpu.CompilerParams(vmem_limit_bytes=16 * 1024 * 1024),
        cost_estimate=pl.CostEstimate(
            flops=2 * 2 * 3 * rows * events * heads * DH,
            bytes_accessed=2 * (events * heads * 4 * DH + events * 2 * DH + rows * heads * DH * 6),
            transcendentals=2 * rows * events * heads,
        ),
        name="attend",
    )(table, *pinned(q_a, q_b, onehot, penalty, cache))


def finish_kernel(heads, parts, part, own, arrived, gates, w_out, sent, kept):
    columns = []
    for h in range(heads):
        at = slice(h * DH, (h + 1) * DH)
        value = own[:, at] + arrived[:, at].astype(jnp.float32)
        scale = lax.rsqrt(jnp.mean(value * value, axis=1, keepdims=True) + norm_eps)
        columns.append((value * scale * gates[:, at].astype(jnp.float32)).astype(jnp.bfloat16))
    hidden = jnp.concatenate(columns, axis=1)
    width = w_out.shape[1] // parts
    for m in range(parts):
        start = pl.multiple_of((part[0] ^ m) * width, width)
        term = jnp.dot(hidden, w_out[:, pl.ds(start, width)], preferred_element_type=jnp.float32)
        if m % 2:
            sent[m // 2] = term.astype(jnp.bfloat16)
        else:
            kept[m // 2] = term


def finish(part, own, arrived, gates, w_out, heads, parts):
    rows = own.shape[0]
    width = w_out.shape[1] // parts
    return pl.pallas_call(
        functools.partial(finish_kernel, heads, parts),
        out_shape=(
            jax.ShapeDtypeStruct((parts // 2, rows, width), jnp.bfloat16),
            jax.ShapeDtypeStruct((parts // 2, rows, width), jnp.float32),
        ),
        in_specs=[SMEM] + [VMEM] * 4,
        out_specs=(VMEM, VMEM),
        compiler_params=pltpu.CompilerParams(vmem_limit_bytes=16 * 1024 * 1024),
        cost_estimate=pl.CostEstimate(
            flops=2 * rows * heads * DH * width * parts,
            bytes_accessed=rows * width * parts * 3,
            transcendentals=rows,
        ),
        name="finish",
    )(part, *pinned(own, arrived, gates, w_out))


def per_device(
    cand_feats, w_in, w_out, kv_cache, event_mask, block_counts, user_blocks, send_slots, cand_user
):
    row_count, slice_width = cand_feats.shape
    heads = w_out.shape[0] // DH
    peers = lax.axis_size("user")
    parts = lax.axis_size("tp")
    cap = send_slots.shape[1]
    me = lax.axis_index("user")
    part = lax.axis_index("tp")
    part_ref = part.reshape(1)
    half = row_count // 2

    order = ring_order(peers)
    place = [0] * peers
    for position, index in enumerate(order):
        place[index] = position
    here = jnp.array(place, jnp.int32)[me]
    onward = [(order[i], order[(i + 1) % peers]) for i in range(peers)]
    back = [(b, a) for a, b in onward]

    def swap(value, axis, bit):
        return lax.ppermute(value, axis, [(i, i ^ bit) for i in range(lax.axis_size(axis))])

    def bits(count):
        return [1 << b for b in range(count.bit_length() - 1)]

    slices = {0: cand_feats}
    for bit in reversed(bits(parts)):
        slices.update({m | bit: swap(value, "tp", bit) for m, value in list(slices.items())})
    slices = [slices[m] for m in range(parts)]

    slot_users = owner_users(block_counts, user_blocks, peers * cap)
    facts = jnp.concatenate([cand_user, slot_users])[None]
    for bit in bits(peers):
        facts = jnp.concatenate([facts, swap(facts, "user", bit)], axis=0)
    users, owners = facts[:, :row_count], facts[:, row_count:]
    labels = jnp.arange(DH, dtype=jnp.int32)
    onehot = (users[:, :, None] == labels).astype(jnp.bfloat16)
    steps = jnp.arange(peers, dtype=jnp.int32)
    slots = send_slots[me ^ steps]
    live = event_mask[slots.reshape(-1)].reshape(peers, cap, EVENTS) > 0
    my_owners = lax.dynamic_slice_in_dim(owners, me * cap, cap, 1)
    label = jnp.where(live, my_owners[:, :, None], -1).reshape(peers, cap * EVENTS)
    penalty = jnp.where(label[:, :, None] == labels, 0.0, MASKED).astype(jnp.bfloat16)

    sequence = jnp.array(order, jnp.int32)
    met = jnp.stack([sequence[(here - steps) % peers], sequence[(here + steps) % peers]], axis=1)
    tables = jnp.concatenate([met ^ me, send_slots[met].reshape(peers, 2 * cap)], axis=1)

    queries = project(part_ref, slices, w_in, heads, 0)
    gates = project(part_ref, slices, w_in, heads, 1)

    def score(step, q_a, q_b):
        return attend(tables[step], q_a, q_b, onehot, penalty, kv_cache, heads, cap)

    q_a, q_b = queries[:half], queries[half:]
    own_a, own_b = score(0, q_a, q_b)
    tables, own_a, own_b = lax.optimization_barrier((tables, own_a, own_b))
    sum_a = sum_b = None
    for step in range(1, peers):
        q_a = lax.ppermute(q_a, "user", onward)
        q_b = lax.ppermute(q_b, "user", back)
        term_a, term_b = score(step, q_a, q_b)
        if sum_a is not None:
            term_a += sum_a.astype(jnp.float32)
            term_b += sum_b.astype(jnp.float32)
        sum_a = lax.ppermute(term_a.astype(jnp.bfloat16), "user", onward)
        sum_b = lax.ppermute(term_b.astype(jnp.bfloat16), "user", back)

    scored = []
    for own, arrived, begin in ((own_a, sum_a, 0), (own_b, sum_b, half)):
        rows = slice(begin, begin + half)
        sent, kept = finish(part_ref, own, arrived, gates[rows], w_out, heads, parts)
        for bit in bits(parts):
            total = kept + swap(sent, "tp", bit).astype(jnp.float32)
            sent, kept = total[1::2].astype(jnp.bfloat16), total[::2]
        scored.append((cand_feats[rows].astype(jnp.float32) + total[0]).astype(jnp.bfloat16))
    return jnp.concatenate(scored, axis=0)


def solution(mesh):
    in_specs = (
        P("user", "tp"),
        P(None, "tp"),
        P("tp", None),
        P("user", None, "tp"),
        P("user", None),
        P("user"),
        P("user", None),
        P("user", None),
        P("user"),
    )
    out_specs = P("user", "tp")
    return jax.shard_map(
        per_device, mesh=mesh, in_specs=in_specs, out_specs=out_specs, check_vma=False
    )
```

```python
import functools

import jax
import jax.numpy as jnp
import numpy as np
from jax import lax
from jax.experimental import pallas as pl
from jax.experimental.pallas import tpu as pltpu
from jax.sharding import PartitionSpec as P

DH = 128
EVENTS = 128
norm_eps = 1e-06
MASKED = -1e30
FACT_ROWS = 16

VMEM = pl.BlockSpec(memory_space=pltpu.VMEM)
SMEM = pl.BlockSpec(memory_space=pltpu.SMEM)


def pin(value):
    return pltpu.with_memory_space_constraint(value, pltpu.VMEM)


def in_hbm(value):
    return pltpu.with_memory_space_constraint(value, pltpu.HBM)


def ring_order(count):
    wide = 1
    while 4 * wide * wide <= count:
        wide *= 2
    deep = count // wide
    order = [z * wide for z in range(deep)]
    for turn, z in enumerate(reversed(range(deep))):
        across = range(1, wide) if turn % 2 == 0 else reversed(range(1, wide))
        order += [z * wide + x for x in across]
    return order


def owner_users(block_count, block_table, slot_count):
    user_count, most_blocks = block_table.shape
    live_mask = jnp.arange(most_blocks, dtype=jnp.int32)[None, :] < block_count[:, None]
    slot_hit = (
        block_table[:, :, None] == jnp.arange(slot_count, dtype=jnp.int32)[None, None, :]
    ) & live_mask[:, :, None]
    user_label = jnp.arange(user_count, dtype=jnp.int32)[:, None, None] + 1
    return jnp.sum(jnp.where(slot_hit, user_label, 0), axis=(0, 1)) - 1


def silu(value):
    return value * (0.5 + 0.5 * jnp.tanh(0.5 * value))


def near_kernel(first, second, mate, w_in, cache, partial, w_here, cache_here, sems):
    copies = [
        pltpu.make_async_copy(source, target, sems.at[i])
        for i, (source, target) in enumerate(((w_in, w_here), (cache, cache_here)))
    ]
    for copy in copies:
        copy.start()
    copies[0].wait()
    half, width = first.shape
    part = lax.axis_index("tp")
    own, other = (
        w_here[pl.ds(pl.multiple_of((part ^ m) * width, width), width)] for m in range(2)
    )
    for begin, piece in ((0, first), (half, second)):
        rows = slice(begin, begin + half)
        partial[rows] = jnp.dot(
            piece[...], own, preferred_element_type=jnp.float32
        ) + jnp.dot(mate[rows], other, preferred_element_type=jnp.float32)
    copies[1].wait()


def near(first, second, mate, w_in, cache):
    rows, width = mate.shape
    hbm = pl.BlockSpec(memory_space=pltpu.HBM)
    held = [jax.ShapeDtypeStruct(value.shape, value.dtype) for value in (w_in, cache)]
    return pl.pallas_call(
        near_kernel,
        out_shape=(jax.ShapeDtypeStruct((rows, w_in.shape[1]), jnp.float32), *held),
        in_specs=[VMEM] * 3 + [hbm] * 2,
        out_specs=(VMEM,) * 3,
        scratch_shapes=[pltpu.SemaphoreType.DMA((2,))],
        compiler_params=pltpu.CompilerParams(vmem_limit_bytes=8 * 1024 * 1024),
        cost_estimate=pl.CostEstimate(
            flops=4 * rows * width * w_in.shape[1],
            bytes_accessed=4 * rows * w_in.shape[1] + 2 * cache.size,
            transcendentals=0,
        ),
        name="near",
    )(pin(first), pin(second), pin(mate), in_hbm(w_in), in_hbm(cache))


def project_kernel(heads, gate, begin, first, partial, *refs):
    slices, (w_in, facts, out) = refs[:-3], refs[-3:]
    rows, width = slices[0].shape
    part = lax.axis_index("tp")
    for h in range(heads):
        column = (2 * h + gate) * DH
        total = partial[begin : begin + rows, column : column + DH]
        for m, piece in enumerate(slices):
            start = pl.multiple_of((part ^ (m + first)) * width, width)
            total += jnp.dot(
                piece[...],
                w_in[pl.ds(start, width), column : column + DH],
                preferred_element_type=jnp.float32,
            )
        out[:rows, h * DH : (h + 1) * DH] = silu(total).astype(jnp.bfloat16)
    if not gate:
        out[rows:] = facts[...]


def project(partial, slices, w_in, facts, heads, gate, begin, first):
    rows = slices[0].shape[0]
    return pl.pallas_call(
        functools.partial(project_kernel, heads, gate, begin, first),
        out_shape=jax.ShapeDtypeStruct(
            (rows + (0 if gate else FACT_ROWS), heads * DH), jnp.bfloat16
        ),
        in_specs=[VMEM] * (len(slices) + 3),
        out_specs=VMEM,
        compiler_params=pltpu.CompilerParams(vmem_limit_bytes=8 * 1024 * 1024),
        name="gates" if gate else "queries",
    )(pin(partial), *[pin(piece) for piece in slices], pin(w_in), pin(facts))


def attend_kernel(heads, cap, step, begin, route, slots, event_mask, q, cache, out):
    rows, width = out.shape
    me = lax.axis_index("user")
    index = route[me, step]
    labels = lax.broadcasted_iota(jnp.int32, (DH, EVENTS), 0)

    facts = q[rows:].astype(jnp.float32).astype(jnp.int32)
    hot = []
    for row in range(begin, begin + rows, EVENTS):
        line, at = divmod(row, width)
        user = facts[line : line + 1, at : at + EVENTS]
        hot.append(jnp.where(user == labels, 1.0, 0.0).T.astype(jnp.bfloat16))
    hot = jnp.concatenate(hot, axis=0)

    line = 2 * rows // width
    owners = facts[line : line + 1, :DH]
    lanes = lax.broadcasted_iota(jnp.int32, (1, DH), 1)
    penalty = []
    for c in range(cap):
        owner = jnp.sum(jnp.where(lanes == me * cap + c, owners, 0), axis=1, keepdims=True)
        live = event_mask[pl.ds(slots[index, c], 1)] > 0
        label = jnp.where(live, owner, -1)
        penalty.append(jnp.where(label == labels, 0.0, MASKED).T.astype(jnp.bfloat16))

    per = min(2, cap)
    for h in range(heads):
        left = jnp.concatenate([q[:rows, h * DH : (h + 1) * DH], hot], axis=1)
        total = None
        for c in range(0, cap, per):
            held = [cache.at[slots[index, c + i]] for i in range(per)]
            keys = jnp.concatenate([b[:, 2 * h * DH : (2 * h + 1) * DH] for b in held], axis=0)
            values = jnp.concatenate(
                [b[:, (2 * h + 1) * DH : (2 * h + 2) * DH] for b in held], axis=0
            )
            right = jnp.concatenate([keys, jnp.concatenate(penalty[c : c + per], axis=0)], axis=1)
            half = lax.dot_general(
                left, right, (((1,), (1,)), ((), ())), preferred_element_type=jnp.float32
            ) * (0.5 * DH ** (-0.5))
            weights = (half + half * jnp.tanh(half)).astype(jnp.bfloat16)
            term = jnp.dot(weights, values, preferred_element_type=jnp.float32)
            total = term if total is None else total + term
        out[:, h * DH : (h + 1) * DH] = total


def attend(step, begin, route, slots, event_mask, q, cache, heads, cap):
    rows = q.shape[0] - FACT_ROWS
    return pl.pallas_call(
        functools.partial(attend_kernel, heads, cap, step, begin),
        out_shape=jax.ShapeDtypeStruct((rows, heads * DH), jnp.float32),
        in_specs=[SMEM] * 2 + [VMEM] * 3,
        out_specs=VMEM,
        compiler_params=pltpu.CompilerParams(vmem_limit_bytes=8 * 1024 * 1024),
        name="attend",
    )(route, slots, pin(event_mask), pin(q), pin(cache))


def finish_kernel(heads, parts, own, arrived, gates, w_out, sent, kept):
    part = lax.axis_index("tp")
    columns = []
    for h in range(heads):
        at = slice(h * DH, (h + 1) * DH)
        value = own[:, at] + arrived[:, at].astype(jnp.float32)
        scale = lax.rsqrt(jnp.mean(value * value, axis=1, keepdims=True) + norm_eps)
        columns.append((value * scale * gates[:, at].astype(jnp.float32)).astype(jnp.bfloat16))
    hidden = jnp.concatenate(columns, axis=1)
    width = w_out.shape[1] // parts
    for m in range(parts):
        start = pl.multiple_of((part ^ m) * width, width)
        term = jnp.dot(hidden, w_out[:, pl.ds(start, width)], preferred_element_type=jnp.float32)
        if m % 2:
            sent[m // 2] = term.astype(jnp.bfloat16)
        else:
            kept[m // 2] = term


def finish(own, arrived, gates, w_out, heads, parts):
    rows = own.shape[0]
    width = w_out.shape[1] // parts
    return pl.pallas_call(
        functools.partial(finish_kernel, heads, parts),
        out_shape=(
            jax.ShapeDtypeStruct((parts // 2, rows, width), jnp.bfloat16),
            jax.ShapeDtypeStruct((parts // 2, rows, width), jnp.float32),
        ),
        in_specs=[VMEM] * 4,
        out_specs=(VMEM, VMEM),
        compiler_params=pltpu.CompilerParams(vmem_limit_bytes=8 * 1024 * 1024),
        name="finish",
    )(pin(own), pin(arrived), pin(gates), pin(w_out))


def per_device(
    cand_feats, w_in, w_out, kv_cache, event_mask, block_counts, user_blocks, send_slots, cand_user
):
    row_count, slice_width = cand_feats.shape
    heads = w_out.shape[0] // DH
    peers = lax.axis_size("user")
    parts = lax.axis_size("tp")
    cap = send_slots.shape[1]
    half = row_count // 2

    order = ring_order(peers)
    route = np.zeros((peers, peers), np.int32)
    for position, index in enumerate(order):
        route[index] = [order[(position - step) % peers] for step in range(peers)]
    route = jnp.array(route)
    onward = [(order[i], order[(i + 1) % peers]) for i in range(peers)]
    back = [(b, a) for a, b in onward]

    def swap(value, axis, bit):
        return lax.ppermute(value, axis, [(i, i ^ bit) for i in range(lax.axis_size(axis))])

    def bits(count):
        return [1 << b for b in range(count.bit_length() - 1)]

    begins = (half, 0)
    width = heads * DH
    slot_users = owner_users(block_counts, user_blocks, peers * cap)
    users = cand_user.reshape(-1, width)
    owners = jnp.pad(slot_users, (0, width - peers * cap))[None]
    facts = jnp.concatenate([users, owners], axis=0).astype(jnp.bfloat16)
    facts = jnp.pad(facts, ((0, FACT_ROWS - facts.shape[0]), (0, 0)))

    rows = {begin: cand_feats[begin : begin + half] for begin in begins}
    mate, facts = lax.optimization_barrier((swap(cand_feats, "tp", 1), facts))
    partial, w_in, cache = near(rows[0], rows[half], mate, w_in, kv_cache)
    queries, gates = {}, {}
    last = partial
    for begin in begins:
        far = {0: rows[begin]}
        if begin != begins[0]:
            far, _ = lax.optimization_barrier((far, partial))
        for bit in reversed(bits(parts)[1:]):
            far.update({m | bit: swap(value, "tp", bit) for m, value in far.items()})
        del far[0]
        far, last = lax.optimization_barrier((far, last))
        far.update({m | 1: swap(value, "tp", 1) for m, value in far.items()})
        far = [far[m] for m in range(2, parts)]
        queries[begin] = project(partial, far, w_in, facts, heads, 0, begin, 2)
        gates[begin] = project(partial, far, w_in, facts, heads, 1, begin, 2)
        last = queries[begin]

    def score(step, begin, query):
        return attend(step, begin, route, send_slots, event_mask, query, cache, heads, cap)

    way = {0: onward, half: back}
    queries_at = {begin: [queries[begin]] for begin in begins}
    for begin in begins:
        for step in range(1, peers):
            queries_at[begin].append(lax.ppermute(queries_at[begin][-1], "user", way[begin]))
    own, sums = {}, {}
    last = None
    turns = [(step, begin) for step in range(1, peers) for begin in begins]
    turns[5:5] = [(0, half)]
    turns[8:8] = [(0, 0)]
    for step, begin in turns:
        query = queries_at[begin][step]
        if last is not None:
            query, last = lax.optimization_barrier((query, last))
        last = term = score(step if begin == 0 else (peers - step) % peers, begin, query)
        if step == 0:
            own[begin] = term
            continue
        if begin in sums:
            term = term + sums[begin].astype(jnp.float32)
        sums[begin] = lax.ppermute(term.astype(jnp.bfloat16), "user", way[begin])

    scored = {}
    for begin in begins:
        sent, kept = finish(own[begin], sums[begin], gates[begin], w_out, heads, parts)
        for bit in bits(parts):
            total = kept + swap(sent, "tp", bit).astype(jnp.float32)
            sent, kept = total[1::2].astype(jnp.bfloat16), total[::2]
        scored[begin] = (rows[begin].astype(jnp.float32) + total[0]).astype(jnp.bfloat16)
    return jnp.concatenate([scored[0], scored[half]], axis=0)


def solution(mesh):
    in_specs = (
        P("user", "tp"),
        P(None, "tp"),
        P("tp", None),
        P("user", None, "tp"),
        P("user", None),
        P("user"),
        P("user", None),
        P("user", None),
        P("user"),
    )
    out_specs = P("user", "tp")
    return jax.shard_map(
        per_device, mesh=mesh, in_specs=in_specs, out_specs=out_specs, check_vma=False
    )
```

```python
import functools

import jax
import jax.numpy as jnp
from jax import lax
from jax.experimental import pallas as pl
from jax.experimental.pallas import tpu as pltpu
from jax.sharding import PartitionSpec as P

DH = 128
EVENTS = 128
norm_eps = 1e-06
MASKED = -1e30
FACT_ROWS = 16

VMEM = pl.BlockSpec(memory_space=pltpu.VMEM)
SMEM = pl.BlockSpec(memory_space=pltpu.SMEM)


def pin(value):
    return pltpu.with_memory_space_constraint(value, pltpu.VMEM)


def in_hbm(value):
    return pltpu.with_memory_space_constraint(value, pltpu.HBM)


def ring_order(count):
    wide = 1
    while 4 * wide * wide <= count:
        wide *= 2
    deep = count // wide
    order = [z * wide for z in range(deep)]
    for turn, z in enumerate(reversed(range(deep))):
        across = range(1, wide) if turn % 2 == 0 else reversed(range(1, wide))
        order += [z * wide + x for x in across]
    return order


def owner_users(block_count, block_table, slot_count):
    user_count, most_blocks = block_table.shape
    live_mask = jnp.arange(most_blocks, dtype=jnp.int32)[None, :] < block_count[:, None]
    slot_hit = (
        block_table[:, :, None] == jnp.arange(slot_count, dtype=jnp.int32)[None, None, :]
    ) & live_mask[:, :, None]
    user_label = jnp.arange(user_count, dtype=jnp.int32)[:, None, None] + 1
    return jnp.sum(jnp.where(slot_hit, user_label, 0), axis=(0, 1)) - 1


def silu(value):
    return value * (0.5 + 0.5 * jnp.tanh(0.5 * value))


def near_kernel(
    slots, feats, mate, w_in, cache, event_mask, partial, w_here, cache_here, live, sems
):
    peers, cap = slots.shape
    copies = [pltpu.make_async_copy(w_in, w_here, sems.at[peers * cap])]
    for i in range(peers * cap):
        slot = slots[i // cap, i % cap]
        copies.append(pltpu.make_async_copy(cache.at[slot], cache_here.at[i], sems.at[i]))
    for copy in copies:
        copy.start()
    for i in range(peers * cap):
        live[i : i + 1] = event_mask[pl.ds(slots[i // cap, i % cap], 1)]
    copies[0].wait()
    width = feats.shape[1]
    part = lax.axis_index("tp")
    total = None
    for m, piece in enumerate((feats, mate)):
        start = pl.multiple_of((part ^ m) * width, width)
        term = jnp.dot(
            piece[...], w_here[pl.ds(start, width)], preferred_element_type=jnp.float32
        )
        total = term if total is None else total + term
    partial[...] = total
    for copy in copies[1:]:
        copy.wait()


def near(slots, feats, mate, w_in, cache, event_mask):
    rows, width = mate.shape
    hbm = pl.BlockSpec(memory_space=pltpu.HBM)
    held = [jax.ShapeDtypeStruct(value.shape, value.dtype) for value in (w_in, cache, event_mask)]
    return pl.pallas_call(
        near_kernel,
        out_shape=(jax.ShapeDtypeStruct((rows, w_in.shape[1]), jnp.float32), *held),
        in_specs=[SMEM] + [VMEM] * 2 + [hbm] * 2 + [VMEM],
        out_specs=(VMEM,) * 4,
        scratch_shapes=[pltpu.SemaphoreType.DMA((cache.shape[0] + 1,))],
        compiler_params=pltpu.CompilerParams(vmem_limit_bytes=8 * 1024 * 1024),
        cost_estimate=pl.CostEstimate(
            flops=4 * rows * width * w_in.shape[1],
            bytes_accessed=4 * rows * w_in.shape[1] + 2 * cache.size,
            transcendentals=0,
        ),
        name="near",
    )(slots, pin(feats), pin(mate), in_hbm(w_in), in_hbm(cache), pin(event_mask))


def project_kernel(heads, gate, begin, first, partial, *refs):
    slices, (w_in, facts, out) = refs[:-3], refs[-3:]
    rows, width = partial.shape[0] // 2, slices[0].shape[1]
    part = lax.axis_index("tp")
    for h in range(heads):
        column = (2 * h + gate) * DH
        total = partial[begin : begin + rows, column : column + DH]
        for m, piece in enumerate(slices):
            start = pl.multiple_of((part ^ (m + first)) * width, width)
            total += jnp.dot(
                piece[begin : begin + rows],
                w_in[pl.ds(start, width), column : column + DH],
                preferred_element_type=jnp.float32,
            )
        out[:rows, h * DH : (h + 1) * DH] = silu(total).astype(jnp.bfloat16)
    if not gate:
        out[rows:] = facts[...]


def project(partial, slices, w_in, facts, heads, gate, begin, rows, first):
    return pl.pallas_call(
        functools.partial(project_kernel, heads, gate, begin, first),
        out_shape=jax.ShapeDtypeStruct(
            (rows + (0 if gate else FACT_ROWS), heads * DH), jnp.bfloat16
        ),
        in_specs=[VMEM] * (len(slices) + 3),
        out_specs=VMEM,
        compiler_params=pltpu.CompilerParams(vmem_limit_bytes=8 * 1024 * 1024),
        name="gates" if gate else "queries",
    )(pin(partial), *[pin(piece) for piece in slices], pin(w_in), pin(facts))


def attend_kernel(heads, cap, begin, met, live, q, cache, out):
    rows, width = out.shape
    me = lax.axis_index("user")
    index = sum(jnp.where(me == place, other, 0) for place, other in enumerate(met))
    labels = lax.broadcasted_iota(jnp.int32, (DH, EVENTS), 0)

    facts = q[rows:].astype(jnp.float32).astype(jnp.int32)
    hot = []
    for row in range(begin, begin + rows, EVENTS):
        line, at = divmod(row, width)
        user = facts[line : line + 1, at : at + EVENTS]
        hot.append(jnp.where(user == labels, 1.0, 0.0).T.astype(jnp.bfloat16))
    hot = jnp.concatenate(hot, axis=0)

    line = 2 * rows // width
    owners = facts[line : line + 1, :DH]
    lanes = lax.broadcasted_iota(jnp.int32, (1, DH), 1)
    events = live[index]
    penalty = []
    for c in range(cap):
        owner = jnp.sum(jnp.where(lanes == me * cap + c, owners, 0), axis=1, keepdims=True)
        label = jnp.where(events[c : c + 1] > 0, owner, -1)
        penalty.append(jnp.where(label == labels, 0.0, MASKED).T.astype(jnp.bfloat16))

    per = min(2, cap)
    for h in range(heads):
        left = jnp.concatenate([q[:rows, h * DH : (h + 1) * DH], hot], axis=1)
        total = None
        for c in range(0, cap, per):
            held = [cache.at[index * cap + c + i] for i in range(per)]
            keys = jnp.concatenate([b[:, 2 * h * DH : (2 * h + 1) * DH] for b in held], axis=0)
            values = jnp.concatenate(
                [b[:, (2 * h + 1) * DH : (2 * h + 2) * DH] for b in held], axis=0
            )
            right = jnp.concatenate([keys, jnp.concatenate(penalty[c : c + per], axis=0)], axis=1)
            half = lax.dot_general(
                left, right, (((1,), (1,)), ((), ())), preferred_element_type=jnp.float32
            ) * (0.5 * DH ** (-0.5))
            weights = (half + half * jnp.tanh(half)).astype(jnp.bfloat16)
            term = jnp.dot(weights, values, preferred_element_type=jnp.float32)
            total = term if total is None else total + term
        out[:, h * DH : (h + 1) * DH] = total


def attend(begin, met, live, q, cache, heads, cap):
    rows = q.shape[0] - FACT_ROWS
    return pl.pallas_call(
        functools.partial(attend_kernel, heads, cap, begin, met),
        out_shape=jax.ShapeDtypeStruct((rows, heads * DH), jnp.float32),
        in_specs=[VMEM] * 3,
        out_specs=VMEM,
        compiler_params=pltpu.CompilerParams(vmem_limit_bytes=8 * 1024 * 1024),
        name="attend",
    )(pin(live), pin(q), pin(cache))


def finish_kernel(heads, parts, own, arrived, gates, w_out, sent, kept):
    part = lax.axis_index("tp")
    columns = []
    for h in range(heads):
        at = slice(h * DH, (h + 1) * DH)
        value = own[:, at] + arrived[:, at].astype(jnp.float32)
        scale = lax.rsqrt(jnp.mean(value * value, axis=1, keepdims=True) + norm_eps)
        columns.append((value * scale * gates[:, at].astype(jnp.float32)).astype(jnp.bfloat16))
    hidden = jnp.concatenate(columns, axis=1)
    width = w_out.shape[1] // parts
    for m in range(parts):
        start = pl.multiple_of((part ^ m) * width, width)
        term = jnp.dot(hidden, w_out[:, pl.ds(start, width)], preferred_element_type=jnp.float32)
        if m % 2:
            sent[m // 2] = term.astype(jnp.bfloat16)
        else:
            kept[m // 2] = term


def finish(own, arrived, gates, w_out, heads, parts):
    rows = own.shape[0]
    width = w_out.shape[1] // parts
    return pl.pallas_call(
        functools.partial(finish_kernel, heads, parts),
        out_shape=(
            jax.ShapeDtypeStruct((parts // 2, rows, width), jnp.bfloat16),
            jax.ShapeDtypeStruct((parts // 2, rows, width), jnp.float32),
        ),
        in_specs=[VMEM] * 4,
        out_specs=(VMEM, VMEM),
        compiler_params=pltpu.CompilerParams(vmem_limit_bytes=8 * 1024 * 1024),
        name="finish",
    )(pin(own), pin(arrived), pin(gates), pin(w_out))


def per_device(
    cand_feats, w_in, w_out, kv_cache, event_mask, block_counts, user_blocks, send_slots, cand_user
):
    row_count, slice_width = cand_feats.shape
    heads = w_out.shape[0] // DH
    peers = lax.axis_size("user")
    parts = lax.axis_size("tp")
    cap = send_slots.shape[1]
    half = row_count // 2

    order = ring_order(peers)
    route = [[0] * peers for _ in range(peers)]
    for position, index in enumerate(order):
        for step in range(peers):
            route[step][index] = order[(position - step) % peers]
    onward = [(order[i], order[(i + 1) % peers]) for i in range(peers)]
    back = [(b, a) for a, b in onward]

    def swap(value, axis, bit):
        return lax.ppermute(value, axis, [(i, i ^ bit) for i in range(lax.axis_size(axis))])

    def bits(count):
        return [1 << b for b in range(count.bit_length() - 1)]

    begins = (half, 0)
    width = heads * DH
    slot_users = owner_users(block_counts, user_blocks, peers * cap)
    users = cand_user.reshape(-1, width)
    owners = jnp.pad(slot_users, (0, width - peers * cap))[None]
    facts = jnp.concatenate([users, owners], axis=0).astype(jnp.bfloat16)
    facts = jnp.pad(facts, ((0, FACT_ROWS - facts.shape[0]), (0, 0)))

    mate, facts = lax.optimization_barrier((swap(cand_feats, "tp", 1), facts))
    partial, w_in, cache, live = near(send_slots, cand_feats, mate, w_in, kv_cache, event_mask)
    live = live.reshape(peers, cap, EVENTS)
    far = {0: cand_feats}
    for bit in reversed(bits(parts)[1:]):
        far.update({m | bit: swap(value, "tp", bit) for m, value in far.items()})
    del far[0]
    far, _ = lax.optimization_barrier((far, partial))
    far.update({m | 1: swap(value, "tp", 1) for m, value in far.items()})
    far = [far[m] for m in range(2, parts)]
    queries, gates = {}, {}
    for begin in begins:
        queries[begin] = project(partial, far, w_in, facts, heads, 0, begin, half, 2)
        gates[begin] = project(partial, far, w_in, facts, heads, 1, begin, half, 2)

    def score(step, begin, query):
        return attend(begin, route[step], live, query, cache, heads, cap)

    way = {0: onward, half: back}
    queries_at = {begin: [queries[begin]] for begin in begins}
    for begin in begins:
        for step in range(1, peers):
            queries_at[begin].append(lax.ppermute(queries_at[begin][-1], "user", way[begin]))
    own, sums = {}, {}
    last = None
    turns = [(step, begin) for step in range(1, peers) for begin in begins]
    turns[5:5] = [(0, half)]
    turns[8:8] = [(0, 0)]
    for step, begin in turns:
        query = queries_at[begin][step]
        if last is not None:
            query, last = lax.optimization_barrier((query, last))
        last = term = score(step if begin == 0 else (peers - step) % peers, begin, query)
        if step == 0:
            own[begin] = term
            continue
        if begin in sums:
            term = term + sums[begin].astype(jnp.float32)
        sums[begin] = lax.ppermute(term.astype(jnp.bfloat16), "user", way[begin])

    scored = {}
    for begin in begins:
        sent, kept = finish(own[begin], sums[begin], gates[begin], w_out, heads, parts)
        for bit in bits(parts):
            total = kept + swap(sent, "tp", bit).astype(jnp.float32)
            sent, kept = total[1::2].astype(jnp.bfloat16), total[::2]
        scored[begin] = (cand_feats[begin : begin + half].astype(jnp.float32) + total[0]).astype(jnp.bfloat16)
    return jnp.concatenate([scored[0], scored[half]], axis=0)


def solution(mesh):
    in_specs = (
        P("user", "tp"),
        P(None, "tp"),
        P("tp", None),
        P("user", None, "tp"),
        P("user", None),
        P("user"),
        P("user", None),
        P("user", None),
        P("user"),
    )
    out_specs = P("user", "tp")
    return jax.shard_map(
        per_device, mesh=mesh, in_specs=in_specs, out_specs=out_specs, check_vma=False
    )
```
